512 devices in a mesh: band: 128 (over x_lo, y, z), row: 4 (over x_hi, core).
Axes of the slice: x: 4 (x_hi: 2, x_lo: 2; x = x_hi * 2 + x_lo), y: 8, z: 8, core: 2. Of those that a mesh axis runs over, the one named last changes fastest.
Arguments:
- impedance: bfloat16 [2, 128, 1536, 1536], P(None, 'band', 'row'), may hold values from -1 to 1, as said below
- excitation: bfloat16 [2, 128, 1536, 256], P(None, 'band', 'row'), may hold values from -6 to 6
- port_gain: float32 [1536], P('row'), may hold values from 0.5 to 2
- port_class: int32 [1536], P('row'), may hold values from 0 to 3
- class_limit: int32 [4], replicated, may hold values from 50 to 300
- harmonic: int32 [128], replicated, may hold values from 0 to 127, each once
Outputs:
- currents: float32 [2, 128, 1536, 256], P(None, 'band', 'row')
The draws below stay inside these ranges and needn't reach their ends.
Inputs may be any that keep to these rules, and one draw needn't show every extreme that they name: Each impedance block is symmetric, its real and its imaginary part alike: impedance[c, k, i, j] = impedance[c, k, j, i]. Each harmonic number 0 .. 127 appears once.
All inputs are finite; a program needn't handle non-finite values.
Results may differ from the reference program's by a relative error of at most 0.009.
Values may be sent and summed in bfloat16 or wider, within the bound.
A program may use at most 64 MiB of HBM per device.

```python
import math
import jax
import jax.numpy as jnp
from jax import lax

P_SIZE = 1536
C = 256
NT = 4
ITERS = 3
K = 128
N_ROW = 4


def draw_impedance(key, part):
    key = jax.random.fold_in(key, 7)

    def one_band(band_index):
        band_key = jax.random.fold_in(key, band_index)
        keys = jax.random.split(band_key, 3)
        raw = jax.random.uniform(keys[0], (2, P_SIZE, P_SIZE), jnp.float32, -1.0, 1.0) * jnp.float32(0.6 / math.sqrt(P_SIZE))
        symmetric = raw + jnp.swapaxes(raw, 1, 2)
        real_diag = jax.random.uniform(keys[1], (P_SIZE,), jnp.float32, 0.3, 0.8)
        imag_diag = jax.random.uniform(keys[2], (P_SIZE,), jnp.float32, 0.2, 0.6)
        identity = jnp.eye(P_SIZE, dtype=jnp.float32)
        symmetric = symmetric + jnp.stack([real_diag, imag_diag])[:, :, None] * identity[None, :, :]
        return symmetric.astype(jnp.bfloat16)
    stacked = lax.map(one_band, jnp.arange(K, dtype=jnp.int32))
    return jnp.swapaxes(stacked, 0, 1)


def with_ends(result, key, least, high):
    longest = result.shape.index(max(result.shape))
    spots = []
    for shift in (0, 1):
        where = [jax.random.randint(jax.random.fold_in(key, axis), (), 0, length) for axis, length in enumerate(result.shape)]
        where[longest] = (where[longest] + shift) % result.shape[longest]
        spots.append(tuple(where))
    return result.at[spots[0]].set(least).at[spots[1]].set(high)


def level_of(own_key, dims, cuts, low, largest):
    gain, own = 1.0, jax.random.fold_in(own_key, 6)
    for axis_at, parts in cuts:
        draws = jnp.exp(jax.random.uniform(jax.random.fold_in(own, axis_at), (parts,), jnp.float32, low / len(cuts), largest / len(cuts)))
        gain = gain * jnp.repeat(draws, dims[axis_at] // parts).reshape([-1 if axis == axis_at else 1 for axis in range(len(dims))])
    return gain


def centred(own_key, extent, width, reach, shards=(), kind=jnp.bfloat16):
    entries = width * jax.random.normal(own_key, extent, jnp.float32)
    if shards:
        entries = entries * level_of(own_key, extent, shards, -0.22, 0.18)
    return jnp.clip(entries, -reach, reach).astype(kind)


def setup_inputs(seed: int = 0) -> dict:
    streams_of = jax.random.split(jax.random.key(seed), 7)
    return {
        "impedance": draw_impedance(jax.random.fold_in(streams_of[6], 71), 0),
        "excitation": centred(streams_of[1], (2, K, P_SIZE, C), 1.0, 6.0, ((1, 128), (2, 4))),
        "port_gain": jnp.clip(jnp.exp(math.log(2.0) - 1.3862944 * jax.random.uniform(streams_of[2], (P_SIZE,), jnp.float32) ** level_of(streams_of[2], (P_SIZE,), ((0, 4),), -0.2, 0.2)), 0.5, 2.0),
        "port_class": with_ends(jax.random.randint(streams_of[3], (P_SIZE,), 0, NT), jax.random.fold_in(streams_of[3], 1), 0, NT - 1).astype(jnp.int32),
        "class_limit": with_ends(jax.random.randint(streams_of[4], (NT,), 50, 301), jax.random.fold_in(streams_of[4], 1), 50, 300).astype(jnp.int32),
        "harmonic": jax.random.permutation(streams_of[5], K).astype(jnp.int32),
    }


RELAXATION = 0.5

def synth_table(harmonic):
    bin_count = harmonic.shape[0]
    samples = 2 * bin_count
    sample_idx = jnp.arange(samples, dtype=jnp.int32)
    phase_idx = sample_idx[:, None] * harmonic[None, :] % samples
    angles = phase_idx.astype(jnp.float32) * jnp.float32(2.0 * math.pi / samples)
    weights = jnp.where(harmonic == 0, jnp.float32(math.sqrt(1.0 / samples)), jnp.float32(math.sqrt(2.0 / samples)))
    return jnp.concatenate([weights[None, :] * jnp.cos(angles), -weights[None, :] * jnp.sin(angles)], axis=1)

def port_limits(port_class, class_limit):
    classes = jnp.arange(class_limit.shape[0], dtype=jnp.int32)
    picked = jnp.where(port_class[:, None] == classes[None, :], class_limit[None, :], 0)
    return lax.optimization_barrier(jnp.sum(picked, axis=1)).astype(jnp.float32) / jnp.float32(100.0)

def converter(voltage, dft_table, gain_values, limit_values):
    stacked = voltage.reshape(voltage.shape[0] * voltage.shape[1], voltage.shape[2] * voltage.shape[3])
    waveform = jnp.dot(dft_table, stacked, precision=lax.Precision.HIGHEST, preferred_element_type=jnp.float32)
    waveform = waveform.reshape(dft_table.shape[0], voltage.shape[2], voltage.shape[3])
    ceiling = limit_values[None, :, None]
    injected = ceiling * jnp.tanh(gain_values[None, :, None] * waveform / ceiling)
    projected = jnp.dot(dft_table.T, injected.reshape(dft_table.shape[0], voltage.shape[2] * voltage.shape[3]), precision=lax.Precision.HIGHEST, preferred_element_type=jnp.float32)
    return projected.reshape(voltage.shape)

def complex_product(z_cols, current_rows):
    real_part = jnp.dot(z_cols[0], current_rows[0], preferred_element_type=jnp.float32) - jnp.dot(z_cols[1], current_rows[1], preferred_element_type=jnp.float32)
    imag_part = jnp.dot(z_cols[0], current_rows[1], preferred_element_type=jnp.float32) + jnp.dot(z_cols[1], current_rows[0], preferred_element_type=jnp.float32)
    return jnp.stack([real_part, imag_part])

def quarter_products(z_band, current_band, quarter):
    running = jnp.zeros((2, z_band.shape[1], current_band.shape[2]), jnp.float32)
    for member in range(z_band.shape[2] // quarter):
        z_cols = z_band[:, :, member * quarter:(member + 1) * quarter]
        rows_block = current_band[:, member * quarter:(member + 1) * quarter, :]
        rounded = lax.optimization_barrier(complex_product(z_cols, rows_block).astype(jnp.bfloat16))
        running = running + rounded.astype(jnp.float32)
    return running

def reference(impedance, excitation, port_gain, port_class, class_limit, harmonic):
    dft_table = synth_table(harmonic)
    limit_values = port_limits(port_class, class_limit)
    quarter = P_SIZE // N_ROW
    currents = jnp.zeros(excitation.shape, jnp.float32)
    for iteration in range(ITERS):
        driving = excitation.astype(jnp.float32)
        if iteration > 0:
            rounded = currents.astype(jnp.bfloat16)

            def one_band(band_index):
                z_band = lax.dynamic_index_in_dim(impedance, band_index, 1, keepdims=False)
                current_band = lax.dynamic_index_in_dim(rounded, band_index, 1, keepdims=False)
                return quarter_products(z_band, current_band, quarter)
            coupled = lax.map(one_band, jnp.arange(K, dtype=jnp.int32))
            driving = driving - jnp.swapaxes(coupled, 0, 1)
        voltage = lax.optimization_barrier(driving.astype(jnp.bfloat16))
        saturated = lax.optimization_barrier(converter(voltage.astype(jnp.float32), dft_table, port_gain, limit_values).astype(jnp.bfloat16))
        currents = currents + RELAXATION * (saturated.astype(jnp.float32) - currents)
    return currents
```

```python
import functools
import math

import jax
import jax.numpy as jnp
from jax import lax
from jax.experimental import pallas as pl
from jax.experimental.pallas import tpu as pltpu
from jax.sharding import PartitionSpec as P

ITERS = 3
RELAXATION = 0.5
MESH = pl.DeviceIdType.MESH
F32, BF16 = jnp.float32, jnp.bfloat16

NB, NY, NZ = 128, 8, 8
QUARTER = 384
PORTS = 3
LANES = 128
CHUNKS = 2
SAMPLES = 256


def dot(a, b):
    return jnp.dot(a, b, preferred_element_type=F32)


def ring_offset(rank):
    return 4 + ((rank + 1) // 2) * (1 - 2 * (rank % 2))


def each_peer(act):
    for total in range(NY + NZ - 1):
        low, high = max(0, total - NZ + 1), min(NY - 1, total)

        def one(rank, _, total=total):
            dy, dz = ring_offset(rank), ring_offset(total - rank)
            act(1, dy, dz)
            if total < NY + NZ - 2:
                act(0, dy, dz)
            return 0

        lax.fori_loop(low, high + 1, one, 0)


def kernel(
    harmonic_ref,
    gain_ref,
    class_ref,
    limit_ref,
    z_hbm,
    e_ref,
    out_ref,
    z_ref,
    fsend,
    frecv,
    bsend,
    brecv,
    ibuf,
    cur,
    tab,
    tab_t,
    perm,
    z_sem,
    fs,
    fr,
    bs,
    br,
    xs,
    xr,
    cs,
    cr,
    gs,
    gr,
):
    band, row = lax.axis_index("band"), lax.axis_index("row")
    xlo, y, z = band // (NY * NZ), (band // NZ) % NY, band % NZ
    xhi, core = row // 2, row % 2
    row_x = (1 - xhi) * 2 + core
    row_c = xhi * 2 + (1 - core)
    row_d = (1 - xhi) * 2 + (1 - core)

    def peer_band(dx, dy, dz):
        return (((xlo + dx) % 2) * NY + (y + dy) % NY) * NZ + (z + dz) % NZ

    barrier = pltpu.get_barrier_semaphore()

    def greet(band_to, row_to):
        pl.semaphore_signal(
            barrier, inc=1, device_id={"band": band_to, "row": row_to}, device_id_type=MESH
        )

    each_peer(lambda dx, dy, dz: greet(peer_band(dx, dy, dz), row))
    greet(band, row_x)
    greet(band, row_c)

    z_copy = pltpu.make_async_copy(z_hbm, z_ref, z_sem)
    z_copy.start()

    a = lax.broadcasted_iota(jnp.int32, (256, 256), 0)
    b = lax.broadcasted_iota(jnp.int32, (256, 256), 1)
    perm[0] = jnp.where(b == (a % 2) * 128 + a // 2, 1.0, 0.0).astype(BF16)
    perm[1] = jnp.where(a == (b % 2) * 128 + b // 2, 1.0, 0.0).astype(BF16)
    cur[...] = jnp.zeros(cur.shape, F32)

    def put_voltage(it, c, block, real, imag):
        mixed = dot(perm[0], jnp.concatenate([real, imag], axis=0)).astype(BF16)
        fsend.at[it, c, pl.ds(block * 128, 128)].reshape(256, LANES)[...] = mixed

    def voltage_of(it, c, lanes):
        @pl.when(it == 0)
        def _():
            for block in range(3):
                rows = pl.ds(block * 128, 128)
                put_voltage(it, c, block, e_ref[0, rows, lanes], e_ref[1, rows, lanes])

        @pl.when(it > 0)
        def _():
            arrived(ibuf.at[it - 1, c, row_c], cr.at[it - 1, c])
            arrived(ibuf.at[it - 1, c, row_d], gr.at[it - 1, c])
            current = ibuf[it - 1, c].reshape(4 * QUARTER, 2 * LANES)
            for block in range(3):
                rows = pl.ds(block * 128, 128)
                by_real = dot(z_ref[0, rows, :], current)
                by_imag = dot(z_ref[1, rows, :], current)
                real = e_ref[0, rows, lanes].astype(F32) - (by_real[:, :LANES] - by_imag[:, LANES:])
                imag = e_ref[1, rows, lanes].astype(F32) - (by_real[:, LANES:] + by_imag[:, :LANES])
                put_voltage(it, c, block, real.astype(BF16), imag.astype(BF16))

    def arrived(ref, sem):
        pltpu.make_async_copy(ref, ref, sem).wait()

    def send_forward(it, c):
        def one(dx, dy, dz):
            to = peer_band(dx, dy, dz)
            pltpu.make_async_remote_copy(
                fsend.at[it, c, pl.ds(to * PORTS, PORTS)],
                frecv.at[it, c, :, band],
                fs.at[it, c],
                fr.at[it, c],
                device_id={"band": to, "row": row},
                device_id_type=MESH,
            ).start()

        each_peer(one)
        pltpu.make_async_copy(
            fsend.at[it, c, pl.ds(band * PORTS, PORTS)], frecv.at[it, c, :, band], fr.at[it, c]
        ).start()

    def send_back(it, c):
        def one(dx, dy, dz):
            to = peer_band(dx, dy, dz)
            pltpu.make_async_remote_copy(
                bsend.at[it, c, :, to],
                brecv.at[it, c, pl.ds(band * PORTS, PORTS)],
                bs.at[it, c],
                br.at[it, c],
                device_id={"band": to, "row": row},
                device_id_type=MESH,
            ).start()

        each_peer(one)
        pltpu.make_async_copy(
            bsend.at[it, c, :, band], brecv.at[it, c, pl.ds(band * PORTS, PORTS)], br.at[it, c]
        ).start()

    def gather_copy(it, c, slot, to, send, recv):
        return pltpu.make_async_remote_copy(
            ibuf.at[it, c, slot],
            ibuf.at[it, c, slot],
            send.at[it, c],
            recv.at[it, c],
            device_id={"band": band, "row": to},
            device_id_type=MESH,
        )

    def make_tables():
        repeat = jnp.where(a[:NB] == b[:NB] // 2, 1.0, 0.0).astype(BF16)
        spread = jnp.broadcast_to(harmonic_ref[...].astype(F32), (8, NB)).astype(BF16)
        slot = dot(spread, repeat)[:1].astype(jnp.int32)
        phase = (a * slot + 64 * (b % 2)) & (SAMPLES - 1)
        weight = jnp.where(slot == 0, math.sqrt(1.0 / SAMPLES), math.sqrt(2.0 / SAMPLES))
        table = weight * jnp.cos(phase.astype(F32) * (2.0 * math.pi / SAMPLES))
        for ref, full in ((tab, table), (tab_t, table.T)):
            top = full.astype(BF16)
            ref[0] = top
            ref[1] = (full - top.astype(F32)).astype(BF16)

    def evaluate(it, c):
        limits, scales = [], []
        for p in range(PORTS):
            port = band * PORTS + p
            kind = class_ref[port]
            hundredths = jnp.int32(0)
            for t in range(4):
                hundredths += jnp.where(kind == t, limit_ref[t], 0)
            limit = jnp.full((1, LANES), hundredths, jnp.int32).astype(F32) / 100.0
            limits.append(limit)
            scales.append(jnp.full((1, LANES), gain_ref[port], F32) / limit)
        limit, scale = jnp.concatenate(limits, axis=1), jnp.concatenate(scales, axis=1)
        x = jnp.concatenate(
            [frecv.at[it, c, p].reshape(SAMPLES, LANES)[...] for p in range(PORTS)], axis=1
        )
        wave = dot(tab[0], x) + dot(tab[1], x)
        injected = limit * jnp.tanh(scale * wave)
        top = injected.astype(BF16)
        rest = (injected - top.astype(F32)).astype(BF16)
        result = (dot(tab_t[0], top) + (dot(tab_t[0], rest) + dot(tab_t[1], top))).astype(BF16)
        for p in range(PORTS):
            bsend.at[it, c, p].reshape(SAMPLES, LANES)[...] = result[:, p * LANES : (p + 1) * LANES]

    def update(it, c, lanes):
        arrived(brecv.at[it, c], br.at[it, c])
        for block in range(3):
            rows = pl.ds(block * 128, 128)
            mixed = brecv.at[it, c, rows].reshape(256, LANES)[...]
            parts = dot(perm[1], mixed)
            saturated = jnp.concatenate([parts[:128], parts[128:]], axis=1)
            old = cur[c, rows, :]
            new = old + RELAXATION * (saturated - old)
            cur[c, rows, :] = new

            @pl.when(it < ITERS - 1)
            def _():
                ibuf[it, c, row, rows, :] = new.astype(BF16)

            @pl.when(it == ITERS - 1)
            def _():
                out_ref[0, rows, lanes] = new[:, :LANES]
                out_ref[1, rows, lanes] = new[:, LANES:]

    def iteration(it, _):
        def forward(c, _):
            voltage_of(it, c, pl.ds(pl.multiple_of(c * LANES, LANES), LANES))

            @pl.when((it == 0) & (c == 0))
            def _():
                pl.semaphore_wait(barrier, NB - 1 + 2)

            send_forward(it, c)
            return 0

        lax.fori_loop(0, CHUNKS, forward, 0)

        @pl.when(it == 0)
        def _():
            make_tables()
            z_copy.wait()

        def middle(c, _):
            arrived(frecv.at[it, c], fr.at[it, c])
            evaluate(it, c)
            send_back(it, c)
            return 0

        lax.fori_loop(0, CHUNKS, middle, 0)

        def finish(c, _):
            update(it, c, pl.ds(pl.multiple_of(c * LANES, LANES), LANES))

            @pl.when(it < ITERS - 1)
            def _():
                gather_copy(it, c, row, row_x, xs, xr).start()
                gather_copy(it, c, row, row_c, cs, cr).start()

            return 0

        lax.fori_loop(0, CHUNKS, finish, 0)

        @pl.when(it < ITERS - 1)
        def _():
            def relay(c, _):
                gather_copy(it, c, row_x, row_x, xs, xr).wait_recv()
                gather_copy(it, c, row_x, row_c, gs, gr).start()
                return 0

            lax.fori_loop(0, CHUNKS, relay, 0)

        return 0

    lax.fori_loop(0, ITERS, iteration, 0)

    def drain(i, _):
        it, c = i // CHUNKS, i % CHUNKS
        sent = fsend.at[it, c, pl.ds(0, (NB - 1) * PORTS)]
        pltpu.make_async_copy(sent, sent, fs.at[it, c]).wait()
        sent = bsend.at[it, c, :, pl.ds(0, NB - 1)]
        pltpu.make_async_copy(sent, sent, bs.at[it, c]).wait()

        @pl.when(it < ITERS - 1)
        def _():
            gather_copy(it, c, row, row_x, xs, xr).wait_send()
            gather_copy(it, c, row, row_c, cs, cr).wait_send()
            gather_copy(it, c, row_x, row_c, gs, gr).wait_send()

        return 0

    lax.fori_loop(0, ITERS * CHUNKS, drain, 0)


def body(impedance, excitation, port_gain, port_class, class_limit, harmonic):
    vmem, smem = pl.BlockSpec(memory_space=pltpu.VMEM), pl.BlockSpec(memory_space=pltpu.SMEM)
    sems = (ITERS, CHUNKS)
    out = pl.pallas_call(
        kernel,
        name="harmonic_balance",
        out_shape=jax.ShapeDtypeStruct((2, QUARTER, CHUNKS * LANES), F32),
        in_specs=[vmem, smem, smem, smem, pl.BlockSpec(memory_space=pl.ANY), vmem],
        out_specs=vmem,
        scratch_shapes=[
            pltpu.VMEM((2, QUARTER, 4 * QUARTER), BF16),
            pltpu.VMEM(sems + (QUARTER, 2, LANES), BF16),
            pltpu.VMEM(sems + (PORTS, NB, 2, LANES), BF16),
            pltpu.VMEM(sems + (PORTS, NB, 2, LANES), BF16),
            pltpu.VMEM(sems + (QUARTER, 2, LANES), BF16),
            pltpu.VMEM((ITERS - 1, CHUNKS, 4, QUARTER, 2 * LANES), BF16),
            pltpu.VMEM((CHUNKS, QUARTER, 2 * LANES), F32),
            pltpu.VMEM((2, SAMPLES, SAMPLES), BF16),
            pltpu.VMEM((2, SAMPLES, SAMPLES), BF16),
            pltpu.VMEM((2, 256, 256), BF16),
            pltpu.SemaphoreType.DMA,
        ]
        + [pltpu.SemaphoreType.DMA(sems)] * 4
        + [pltpu.SemaphoreType.DMA((ITERS - 1, CHUNKS))] * 6,
        compiler_params=pltpu.CompilerParams(
            collective_id=0, has_side_effects=True, vmem_limit_bytes=48 << 20
        ),
    )(
        harmonic.reshape(1, NB),
        port_gain,
        port_class,
        class_limit,
        impedance.reshape(2, QUARTER, 4 * QUARTER),
        excitation.reshape(2, QUARTER, CHUNKS * LANES),
    )
    return out.reshape(excitation.shape)


def solution(mesh):
    placed = (
        P(None, "band", "row", None),
        P(None, "band", "row", None),
        P("row"),
        P("row"),
        P(),
        P(),
    )
    return jax.shard_map(
        body, mesh=mesh, in_specs=placed, out_specs=P(None, "band", "row", None), check_vma=False
    )
```

```python
import functools
import math

import jax
import jax.numpy as jnp
from jax import lax
from jax.experimental import pallas as pl
from jax.experimental.pallas import tpu as pltpu
from jax.sharding import PartitionSpec as P

ITERS = 3
RELAXATION = 0.5
MESH = pl.DeviceIdType.MESH
F32, BF16 = jnp.float32, jnp.bfloat16

NB, NY, NZ = 128, 8, 8
QUARTER = 384
PORTS = 3
LANES = 128
CHUNKS = 2
SAMPLES = 256


def dot(a, b):
    return jnp.dot(a, b, preferred_element_type=F32)


def hops(t):
    dx, dy, dz = t
    return dx + min(dy, NY - dy) + min(dz, NZ - dz)


PEERS = sorted(
    [(x, y, z) for x in range(2) for y in range(NY) for z in range(NZ) if x + y + z],
    key=lambda t: -hops(t),
)


def each_peer(act):
    for t in PEERS:
        act(*t)


def kernel(
    harmonic_hbm,
    gain_hbm,
    class_hbm,
    limit_hbm,
    z_hbm,
    e_hbm,
    out_hbm,
    harmonic_ref,
    gain_ref,
    class_ref,
    limit_ref,
    z_ref,
    e_ref,
    out_ref,
    fsend,
    frecv,
    bsend,
    brecv,
    ibuf,
    cur,
    tab,
    perm,
    total,
    in_sem,
    out_sem,
    fs,
    fr,
    bs,
    br,
    xs,
    xr,
    cs,
    cr,
    gs,
    gr,
):
    band, row = lax.axis_index("band"), lax.axis_index("row")
    xlo, y, z = band // (NY * NZ), (band // NZ) & (NY - 1), band & (NZ - 1)
    xhi, core = row // 2, row & 1
    row_x = (1 - xhi) * 2 + core
    row_c = xhi * 2 + (1 - core)
    row_d = (1 - xhi) * 2 + (1 - core)

    xs_at = [((xlo + d) & 1) * (NY * NZ) for d in range(2)]
    ys_at = [((y + d) & (NY - 1)) * NZ for d in range(NY)]
    zs_at = [(z + d) & (NZ - 1) for d in range(NZ)]

    def peer_band(dx, dy, dz):
        return xs_at[dx] + ys_at[dy] + zs_at[dz]

    e_copy = pltpu.make_async_copy(e_hbm, e_ref, in_sem.at[0])
    small_copies = [
        pltpu.make_async_copy(harmonic_hbm, harmonic_ref, in_sem.at[1]),
        pltpu.make_async_copy(gain_hbm, gain_ref, in_sem.at[2]),
        pltpu.make_async_copy(class_hbm, class_ref, in_sem.at[3]),
        pltpu.make_async_copy(limit_hbm, limit_ref, in_sem.at[4]),
    ]
    z_copy = pltpu.make_async_copy(z_hbm, z_ref, in_sem.at[5])
    e_copy.start()
    for copy in small_copies:
        copy.start()
    z_copy.start()

    barrier = pltpu.get_barrier_semaphore()

    def greet(band_to, row_to):
        pl.semaphore_signal(
            barrier, inc=1, device_id={"band": band_to, "row": row_to}, device_id_type=MESH
        )

    each_peer(lambda dx, dy, dz: greet(peer_band(dx, dy, dz), row))
    greet(band, row_x)
    greet(band, row_c)

    def out_copy(c):
        return pltpu.make_async_copy(
            out_ref.at[c],
            out_hbm.at[:, :, pl.ds(pl.multiple_of(c * LANES, LANES), LANES)],
            out_sem.at[c],
        )

    a = lax.broadcasted_iota(jnp.int32, (256, 256), 0)
    b = lax.broadcasted_iota(jnp.int32, (256, 256), 1)
    perm[0] = jnp.where(b == (a % 2) * 128 + a // 2, 1.0, 0.0).astype(BF16)
    perm[1] = jnp.where(a == (b % 2) * 128 + b // 2, 1.0, 0.0).astype(BF16)
    cur[...] = jnp.zeros(cur.shape, F32)
    e_copy.wait()

    def put_voltage(it, c, block, real, imag):
        mixed = dot(perm[0], jnp.concatenate([real, imag], axis=0)).astype(BF16)
        fsend.at[it, c, pl.ds(block * 128, 128)].reshape(256, LANES)[...] = mixed

    def first_voltage(c):
        lanes = pl.ds(c * LANES, LANES)
        for block in range(3):
            rows = pl.ds(block * 128, 128)
            put_voltage(0, c, block, e_ref[0, rows, lanes], e_ref[1, rows, lanes])

    def next_voltage(it, c):
        lanes = pl.ds(pl.multiple_of(c * LANES, LANES), LANES)

        def add(slot, first):
            current = ibuf[it - 1, c, slot]
            columns = pl.ds(pl.multiple_of(slot * QUARTER, QUARTER), QUARTER)
            for part in range(2):
                term = dot(z_ref[part, :, columns], current)
                total[part] = term if first else total[part] + term

        add(row, True)
        for block in range(3):
            gather_copy(it - 1, c, block, row_c, row_c, cs, cr).wait_recv()
        add(row_c, False)
        for block in range(3):
            gather_copy(it - 1, c, block, row_x, row_x, xs, xr).wait_recv()
            gather_copy(it - 1, c, block, row_x, row_c, gs, gr).start()
        add(row_x, False)
        for block in range(3):
            gather_copy(it - 1, c, block, row_d, row_c, gs, gr).wait_recv()
        add(row_d, False)
        for block in range(3):
            rows = pl.ds(block * 128, 128)
            by_real, by_imag = total[0, rows, :], total[1, rows, :]
            real = e_ref[0, rows, lanes].astype(F32) - (by_real[:, :LANES] - by_imag[:, LANES:])
            imag = e_ref[1, rows, lanes].astype(F32) - (by_real[:, LANES:] + by_imag[:, :LANES])
            put_voltage(it, c, block, real.astype(BF16), imag.astype(BF16))

    def arrived(ref, sem):
        pltpu.make_async_copy(ref, ref, sem).wait()

    def send_forward(it, c):
        def one(dx, dy, dz):
            to = peer_band(dx, dy, dz)
            pltpu.make_async_remote_copy(
                fsend.at[it, c, pl.ds(to * PORTS, PORTS)],
                frecv.at[it, c, :, band],
                fs.at[it, c],
                fr.at[it, c],
                device_id={"band": to, "row": row},
                device_id_type=MESH,
            ).start()

        each_peer(one)
        pltpu.make_async_copy(
            fsend.at[it, c, pl.ds(band * PORTS, PORTS)], frecv.at[it, c, :, band], fr.at[it, c]
        ).start()

    def send_back(it, c):
        def one(dx, dy, dz):
            to = peer_band(dx, dy, dz)
            pltpu.make_async_remote_copy(
                bsend.at[it, c, :, to],
                brecv.at[it, c, pl.ds(band * PORTS, PORTS)],
                bs.at[it, c],
                br.at[it, c],
                device_id={"band": to, "row": row},
                device_id_type=MESH,
            ).start()

        each_peer(one)
        pltpu.make_async_copy(
            bsend.at[it, c, :, band], brecv.at[it, c, pl.ds(band * PORTS, PORTS)], br.at[it, c]
        ).start()

    def gather_copy(it, c, block, slot, to, send, recv):
        rows = pl.ds(block * 128, 128)
        return pltpu.make_async_remote_copy(
            ibuf.at[it, c, slot, rows],
            ibuf.at[it, c, slot, rows],
            send.at[it, c, block],
            recv.at[it, c, block],
            device_id={"band": band, "row": to},
            device_id_type=MESH,
        )

    def make_tables():
        repeat = jnp.where(a[:NB] == b[:NB] // 2, 1.0, 0.0).astype(BF16)
        spread = jnp.broadcast_to(harmonic_ref[...].astype(F32), (8, NB)).astype(BF16)
        slot = dot(spread, repeat)[:1].astype(jnp.int32)
        phase = (a * slot + 64 * (b % 2)) & (SAMPLES - 1)
        weight = jnp.where(slot == 0, math.sqrt(1.0 / SAMPLES), math.sqrt(2.0 / SAMPLES))
        table = weight * jnp.cos(phase.astype(F32) * (2.0 * math.pi / SAMPLES))
        tab[0] = table.astype(BF16)
        tab[1] = table.T.astype(BF16)

    def evaluate(it, c):
        limits, scales = [], []
        for p in range(PORTS):
            port = band * PORTS + p
            kind = class_ref[port]
            hundredths = jnp.int32(0)
            for t in range(4):
                hundredths += jnp.where(kind == t, limit_ref[t], 0)
            limit = jnp.full((1, LANES), hundredths, jnp.int32).astype(F32) / 100.0
            limits.append(limit)
            scales.append(jnp.full((1, LANES), gain_ref[port], F32) / limit)
        limit, scale = jnp.concatenate(limits, axis=1), jnp.concatenate(scales, axis=1)
        x = jnp.concatenate(
            [frecv.at[it, c, p].reshape(SAMPLES, LANES)[...] for p in range(PORTS)], axis=1
        )
        wave = dot(tab[0], x)
        injected = limit * jnp.tanh(scale * wave)
        result = dot(tab[1], injected.astype(BF16)).astype(BF16)
        for p in range(PORTS):
            bsend.at[it, c, p].reshape(SAMPLES, LANES)[...] = result[:, p * LANES : (p + 1) * LANES]

    def update(it, c):
        arrived(brecv.at[it, c], br.at[it, c])
        for block in range(3):
            rows = pl.ds(block * 128, 128)
            mixed = brecv.at[it, c, rows].reshape(256, LANES)[...]
            parts = dot(perm[1], mixed)
            saturated = jnp.concatenate([parts[:128], parts[128:]], axis=1)
            old = cur[c, rows, :]
            new = old + RELAXATION * (saturated - old)
            cur[c, rows, :] = new

            @pl.when(it < ITERS - 1)
            def _():
                ibuf[it, c, row, rows, :] = new.astype(BF16)
                gather_copy(it, c, block, row, row_x, xs, xr).start()
                gather_copy(it, c, block, row, row_c, cs, cr).start()

            @pl.when(it == ITERS - 1)
            def _():
                out_ref[c, 0, rows, :] = new[:, :LANES]
                out_ref[c, 1, rows, :] = new[:, LANES:]

    first_voltage(0)
    pl.semaphore_wait(barrier, NB - 1 + 2)
    send_forward(0, 0)
    first_voltage(1)
    send_forward(0, 1)
    for copy in small_copies:
        copy.wait()
    make_tables()
    z_copy.wait()

    def iteration(it, _):
        def middle(c, _):
            arrived(frecv.at[it, c], fr.at[it, c])
            evaluate(it, c)
            send_back(it, c)
            return 0

        lax.fori_loop(0, CHUNKS, middle, 0)

        def finish(c, _):
            update(it, c)

            @pl.when(it == ITERS - 1)
            def _():
                out_copy(c).start()

            return 0

        lax.fori_loop(0, CHUNKS, finish, 0)

        @pl.when(it < ITERS - 1)
        def _():
            def forward(c, _):
                next_voltage(it + 1, c)
                send_forward(it + 1, c)
                return 0

            lax.fori_loop(0, CHUNKS, forward, 0)


        return 0

    lax.fori_loop(0, ITERS, iteration, 0)

    def drain(i, _):
        it, c = i // CHUNKS, i % CHUNKS
        sent = fsend.at[it, c, pl.ds(0, (NB - 1) * PORTS)]
        pltpu.make_async_copy(sent, sent, fs.at[it, c]).wait()
        sent = bsend.at[it, c, :, pl.ds(0, NB - 1)]
        pltpu.make_async_copy(sent, sent, bs.at[it, c]).wait()

        @pl.when(it < ITERS - 1)
        def _():
            for block in range(3):
                gather_copy(it, c, block, row, row_x, xs, xr).wait_send()
                gather_copy(it, c, block, row, row_c, cs, cr).wait_send()
                gather_copy(it, c, block, row_x, row_c, gs, gr).wait_send()

        return 0

    lax.fori_loop(0, ITERS * CHUNKS, drain, 0)
    for c in range(CHUNKS):
        out_copy(c).wait()


def body(impedance, excitation, port_gain, port_class, class_limit, harmonic):
    sems = (ITERS, CHUNKS)
    out = pl.pallas_call(
        kernel,
        name="harmonic_balance",
        out_shape=jax.ShapeDtypeStruct((2, QUARTER, CHUNKS * LANES), F32),
        in_specs=[pl.BlockSpec(memory_space=pl.ANY)] * 6,
        out_specs=pl.BlockSpec(memory_space=pl.ANY),
        scratch_shapes=[
            pltpu.VMEM((1, NB), jnp.int32),
            pltpu.SMEM((QUARTER,), F32),
            pltpu.SMEM((QUARTER,), jnp.int32),
            pltpu.SMEM((4,), jnp.int32),
            pltpu.VMEM((2, QUARTER, 4 * QUARTER), BF16),
            pltpu.VMEM((2, QUARTER, CHUNKS * LANES), BF16),
            pltpu.VMEM((CHUNKS, 2, QUARTER, LANES), F32),
            pltpu.VMEM(sems + (QUARTER, 2, LANES), BF16),
            pltpu.VMEM(sems + (PORTS, NB, 2, LANES), BF16),
            pltpu.VMEM(sems + (PORTS, NB, 2, LANES), BF16),
            pltpu.VMEM(sems + (QUARTER, 2, LANES), BF16),
            pltpu.VMEM((ITERS - 1, CHUNKS, 4, QUARTER, 2 * LANES), BF16),
            pltpu.VMEM((CHUNKS, QUARTER, 2 * LANES), F32),
            pltpu.VMEM((2, SAMPLES, SAMPLES), BF16),
            pltpu.VMEM((2, 256, 256), BF16),
            pltpu.VMEM((2, QUARTER, 2 * LANES), F32),
            pltpu.SemaphoreType.DMA((6,)),
            pltpu.SemaphoreType.DMA((CHUNKS,)),
        ]
        + [pltpu.SemaphoreType.DMA(sems)] * 4
        + [pltpu.SemaphoreType.DMA((ITERS - 1, CHUNKS, 3))] * 6,
        compiler_params=pltpu.CompilerParams(
            collective_id=0, has_side_effects=True, vmem_limit_bytes=60 << 20
        ),
    )(
        harmonic.reshape(1, NB),
        port_gain,
        port_class,
        class_limit,
        impedance.reshape(2, QUARTER, 4 * QUARTER),
        excitation.reshape(2, QUARTER, CHUNKS * LANES),
    )
    return out.reshape(excitation.shape)


def solution(mesh):
    placed = (
        P(None, "band", "row", None),
        P(None, "band", "row", None),
        P("row"),
        P("row"),
        P(),
        P(),
    )
    return jax.shard_map(
        body, mesh=mesh, in_specs=placed, out_specs=P(None, "band", "row", None), check_vma=False
    )
```

```python
import functools
import math

import jax
import jax.numpy as jnp
from jax import lax
from jax.experimental import pallas as pl
from jax.experimental.pallas import tpu as pltpu
from jax.sharding import PartitionSpec as P

ITERS = 3
RELAXATION = 0.5
MESH = pl.DeviceIdType.MESH
F32, BF16 = jnp.float32, jnp.bfloat16

NB, NY, NZ = 128, 8, 8
QUARTER = 384
PORTS = 3
LANES = 128
PLANE = NY * NZ
HALF = QUARTER // 2
CHUNKS = 2
SAMPLES = 256


def dot(a, b):
    return jnp.dot(a, b, preferred_element_type=F32)


def hops(t):
    dx, dy, dz = t
    return dx + min(dy, NY - dy) + min(dz, NZ - dz)


PEERS = sorted(
    [(x, y, z) for x in range(2) for y in range(NY) for z in range(NZ) if x + y + z],
    key=lambda t: -hops(t),
)


def each_peer(act):
    for t in PEERS:
        act(*t)


def kernel(
    harmonic_hbm,
    gain_hbm,
    class_hbm,
    limit_hbm,
    z_hbm,
    e_hbm,
    old_hbm,
    last_hbm,
    harmonic_ref,
    gain_ref,
    class_ref,
    limit_ref,
    z_ref,
    e_ref,
    last_ref,
    fsend,
    frecv,
    bsend,
    plane,
    brecv,
    across,
    ibuf,
    cur,
    tab,
    mix,
    part,
    total,
    in_sem,
    out_sem,
    fs,
    fr,
    bs,
    br,
    pr,
    xs,
    xr,
    cs,
    cr,
    gs,
    gr,
):
    band, row = lax.axis_index("band"), lax.axis_index("row")
    xlo, y, z = band // (NY * NZ), (band // NZ) & (NY - 1), band & (NZ - 1)
    xhi, core = row // 2, row & 1
    band_o = band + PLANE * (1 - 2 * xlo)
    place = y * NZ + z
    row_x = (1 - xhi) * 2 + core
    row_c = xhi * 2 + (1 - core)
    row_d = (1 - xhi) * 2 + (1 - core)

    xs_at = [(xlo + d) & 1 for d in range(2)]
    ys_at = [((y + d) & (NY - 1)) * NZ for d in range(NY)]
    zs_at = [(z + d) & (NZ - 1) for d in range(NZ)]

    def peer_band(dx, dy, dz):
        return xs_at[dx] * PLANE + ys_at[dy] + zs_at[dz]

    e_copy = pltpu.make_async_copy(e_hbm, e_ref, in_sem.at[0])
    small_copies = [
        pltpu.make_async_copy(harmonic_hbm, harmonic_ref, in_sem.at[1]),
        pltpu.make_async_copy(gain_hbm, gain_ref, in_sem.at[2]),
        pltpu.make_async_copy(class_hbm, class_ref, in_sem.at[3]),
        pltpu.make_async_copy(limit_hbm, limit_ref, in_sem.at[4]),
    ]
    z_copy = pltpu.make_async_copy(z_hbm, z_ref, in_sem.at[5])
    e_copy.start()
    for copy in small_copies:
        copy.start()
    z_copy.start()

    barrier = pltpu.get_barrier_semaphore()

    def greet(band_to, row_to):
        pl.semaphore_signal(
            barrier, inc=1, device_id={"band": band_to, "row": row_to}, device_id_type=MESH
        )

    each_peer(lambda dx, dy, dz: greet(peer_band(dx, dy, dz), row))
    greet(band, row_x)
    greet(band, row_c)
    greet(band_o, row_x)

    def lanes_of(c):
        return pl.ds(pl.multiple_of(c * LANES, LANES), LANES)

    def old_copy(c, half):
        return pltpu.make_async_copy(
            cur.at[c, 0, :, pl.ds(half * LANES, LANES)],
            old_hbm.at[half, :, lanes_of(c)],
            out_sem.at[c, half],
        )

    def last_copy(c):
        return pltpu.make_async_copy(
            last_ref.at[c], last_hbm.at[:, :, lanes_of(c)], out_sem.at[c, 2]
        )

    a = lax.broadcasted_iota(jnp.int32, (256, 256), 0)
    b = lax.broadcasted_iota(jnp.int32, (256, 256), 1)
    mix[...] = jnp.where(b == (a % 2) * 128 + a // 2, 1.0, 0.0).astype(BF16)
    a2, b2 = a[:128, :128], b[:128, :128]
    part[...] = jnp.where(b2 == (a2 % 64) * 2 + a2 // 64, 1.0, 0.0).astype(BF16)
    cur[...] = jnp.zeros(cur.shape, F32)
    e_copy.wait()

    def put_voltage(it, c, block, real, imag):
        mixed = dot(mix[...], jnp.concatenate([real, imag], axis=0)).astype(BF16)
        fsend.at[it, c, pl.ds(block * 128, 128)].reshape(256, LANES)[...] = mixed

    def first_voltage(c):
        lanes = pl.ds(c * LANES, LANES)
        for block in range(3):
            rows = pl.ds(block * 128, 128)
            put_voltage(0, c, block, e_ref[0, rows, lanes], e_ref[1, rows, lanes])

    def next_voltage(it, c):
        lanes = lanes_of(c)

        def add(slot, first):
            current = ibuf[it - 1, c, slot]
            columns = pl.ds(pl.multiple_of(slot * QUARTER, QUARTER), QUARTER)
            for side in range(2):
                term = dot(z_ref[side, :, columns], current)
                total[side] = term if first else total[side] + term

        across_copy(it - 1, c, 0).wait_recv()
        relax(it - 1, c, 0, 1 - xlo, across.at[it - 1, c, 0])
        core_copy(it - 1, c, row, 1 - xlo, cs, cr).start()
        add(row, True)
        across_copy(it - 1, c, 1).wait_recv()
        relax(it - 1, c, 1, 1 - xlo, across.at[it - 1, c, 1])
        core_copy(it - 1, c, row_x, 1 - xlo, gs, gr).start()
        across_copy(it - 1, c, 2).wait_recv()
        relax(it - 1, c, 1, xlo, across.at[it - 1, c, 2])
        core_copy(it - 1, c, row_x, xlo, gs, gr).start()
        add(row_x, False)
        core_copy(it - 1, c, row_c, 0, cs, cr).wait_recv()
        core_copy(it - 1, c, row_c, 1, cs, cr).wait_recv()
        add(row_c, False)
        core_copy(it - 1, c, row_d, 0, gs, gr).wait_recv()
        core_copy(it - 1, c, row_d, 1, gs, gr).wait_recv()
        add(row_d, False)
        for block in range(3):
            rows = pl.ds(block * 128, 128)
            by_real, by_imag = total[0, rows, :], total[1, rows, :]
            real = e_ref[0, rows, lanes].astype(F32) - (by_real[:, :LANES] - by_imag[:, LANES:])
            imag = e_ref[1, rows, lanes].astype(F32) - (by_real[:, LANES:] + by_imag[:, :LANES])
            put_voltage(it, c, block, real.astype(BF16), imag.astype(BF16))

    def arrived(ref, sem):
        pltpu.make_async_copy(ref, ref, sem).wait()

    def send_forward(it, c):
        def one(dx, dy, dz):
            to = peer_band(dx, dy, dz)
            pltpu.make_async_remote_copy(
                fsend.at[it, c, pl.ds(to * PORTS, PORTS)],
                frecv.at[it, c, :, band],
                fs.at[it, c],
                fr.at[it, c],
                device_id={"band": to, "row": row},
                device_id_type=MESH,
            ).start()

        each_peer(one)
        pltpu.make_async_copy(
            fsend.at[it, c, pl.ds(band * PORTS, PORTS)], frecv.at[it, c, :, band], fr.at[it, c]
        ).start()

    def send_back(c):
        it = ITERS - 1

        def one(dx, dy, dz):
            pltpu.make_async_remote_copy(
                bsend.at[it, c, xs_at[dx], :, ys_at[dy] + zs_at[dz]],
                brecv.at[c, pl.ds(band * PORTS, PORTS)],
                bs.at[it, c],
                br.at[c],
                device_id={"band": peer_band(dx, dy, dz), "row": row},
                device_id_type=MESH,
            ).start()

        each_peer(one)
        pltpu.make_async_copy(
            bsend.at[it, c, xlo, :, place], brecv.at[c, pl.ds(band * PORTS, PORTS)], br.at[c]
        ).start()

    def send_plane(it, c):
        mine = plane.at[it, c, :, pl.ds(place * PORTS, PORTS)]

        def one(dx, dy, dz):
            if dx:
                return
            pltpu.make_async_remote_copy(
                bsend.at[it, c, :, :, ys_at[dy] + zs_at[dz]],
                mine,
                bs.at[it, c],
                pr.at[it, c],
                device_id={"band": peer_band(0, dy, dz), "row": row},
                device_id_type=MESH,
            ).start()

        each_peer(one)
        pltpu.make_async_copy(bsend.at[it, c, :, :, place], mine, pr.at[it, c]).start()

    def across_copy(it, c, which):
        return pltpu.make_async_remote_copy(
            plane.at[it, c, xlo if which == 2 else 1 - xlo],
            across.at[it, c, which],
            xs.at[it, c, which],
            xr.at[it, c, which],
            device_id={
                "band": band if which == 2 else band_o,
                "row": row if which == 0 else row_x,
            },
            device_id_type=MESH,
        )

    def core_copy(it, c, slot, half, send, recv):
        rows = pl.ds(pl.multiple_of(half * HALF, HALF), HALF)
        return pltpu.make_async_remote_copy(
            ibuf.at[it, c, slot, rows],
            ibuf.at[it, c, slot, rows],
            send.at[it, c, half],
            recv.at[it, c, half],
            device_id={"band": band, "row": row_c},
            device_id_type=MESH,
        )

    def parted(ref):
        rows = ref.reshape(2 * HALF, LANES)[...]
        return dot(part[...], jnp.concatenate([rows[:128], rows[128:256], rows[256:]], axis=1))

    def relax(it, c, which, half, ref):
        blocks = parted(ref)
        for block in range(3):
            lanes = slice(block * LANES, (block + 1) * LANES)
            saturated = jnp.concatenate([blocks[:64, lanes], blocks[64:, lanes]], axis=1)
            rows = pl.ds(pl.multiple_of(half * HALF + block * 64, 64), 64)
            old = cur[c, which, rows, :]
            new = old + RELAXATION * (saturated - old)
            cur[c, which, rows, :] = new
            ibuf[it, c, row if which == 0 else row_x, rows, :] = new.astype(BF16)

    def make_tables():
        repeat = jnp.where(a[:NB] == b[:NB] // 2, 1.0, 0.0).astype(BF16)
        spread = jnp.broadcast_to(harmonic_ref[...].astype(F32), (8, NB)).astype(BF16)
        slot = dot(spread, repeat)[:1].astype(jnp.int32)
        phase = (a * slot + 64 * (b % 2)) & (SAMPLES - 1)
        weight = jnp.where(slot == 0, math.sqrt(1.0 / SAMPLES), math.sqrt(2.0 / SAMPLES))
        table = weight * jnp.cos(phase.astype(F32) * (2.0 * math.pi / SAMPLES))
        tab[0] = table.astype(BF16)
        tab[1] = table.T.astype(BF16)

    def evaluate(it, c):
        limits, scales = [], []
        for p in range(PORTS):
            port = band * PORTS + p
            kind = class_ref[port]
            hundredths = jnp.int32(0)
            for t in range(4):
                hundredths += jnp.where(kind == t, limit_ref[t], 0)
            limit = jnp.full((1, LANES), hundredths, jnp.int32).astype(F32) / 100.0
            limits.append(limit)
            scales.append(jnp.full((1, LANES), gain_ref[port], F32) / limit)
        limit, scale = jnp.concatenate(limits, axis=1), jnp.concatenate(scales, axis=1)
        x = jnp.concatenate(
            [frecv.at[it, c, p].reshape(SAMPLES, LANES)[...] for p in range(PORTS)], axis=1
        )
        wave = dot(tab[0], x)
        injected = limit * jnp.tanh(scale * wave)
        result = dot(tab[1], injected.astype(BF16)).astype(BF16)
        for p in range(PORTS):
            for to in range(2):
                bsend.at[it, c, to, p].reshape(2 * PLANE, LANES)[...] = result[
                    to * 128 : (to + 1) * 128, p * LANES : (p + 1) * LANES
                ]

    first_voltage(0)
    pl.semaphore_wait(barrier, NB - 1 + 3)
    send_forward(0, 0)
    first_voltage(1)
    send_forward(0, 1)
    for copy in small_copies:
        copy.wait()
    make_tables()
    z_copy.wait()

    def iteration(it, _):
        def middle(c, _):
            arrived(frecv.at[it, c], fr.at[it, c])
            evaluate(it, c)
            send_plane(it, c)
            return 0

        lax.fori_loop(0, CHUNKS, middle, 0)

        def spread(c, _):
            arrived(plane.at[it, c], pr.at[it, c])
            across_copy(it, c, 2).start()
            across_copy(it, c, 0).start()
            across_copy(it, c, 1).start()
            relax(it, c, 0, xlo, plane.at[it, c, xlo])
            core_copy(it, c, row, xlo, cs, cr).start()
            return 0

        lax.fori_loop(0, CHUNKS, spread, 0)

        def forward(c, _):
            next_voltage(it + 1, c)
            send_forward(it + 1, c)
            return 0

        lax.fori_loop(0, CHUNKS, forward, 0)
        return 0

    lax.fori_loop(0, ITERS - 1, iteration, 0)

    for c in range(CHUNKS):
        for half in range(2):
            old_copy(c, half).start()

    def last_middle(c, _):
        arrived(frecv.at[ITERS - 1, c], fr.at[ITERS - 1, c])
        evaluate(ITERS - 1, c)
        send_back(c)
        return 0

    lax.fori_loop(0, CHUNKS, last_middle, 0)

    def finish(c, _):
        arrived(brecv.at[c], br.at[c])
        for half in range(2):
            blocks = parted(brecv.at[c, pl.ds(half * HALF, HALF)]).astype(BF16)
            for block in range(3):
                lanes = slice(block * LANES, (block + 1) * LANES)
                rows = pl.ds(half * HALF + block * 64, 64)
                last_ref[c, 0, rows, :] = blocks[:64, lanes]
                last_ref[c, 1, rows, :] = blocks[64:, lanes]
        last_copy(c).start()
        return 0

    lax.fori_loop(0, CHUNKS, finish, 0)

    def drain(i, _):
        it, c = i // CHUNKS, i % CHUNKS
        sent = fsend.at[it, c, pl.ds(0, (NB - 1) * PORTS)]
        pltpu.make_async_copy(sent, sent, fs.at[it, c]).wait()
        return 0

    def drain_gather(i, _):
        it, c = i // CHUNKS, i % CHUNKS
        sent = bsend.at[it, c, :, :, pl.ds(0, PLANE - 1)]
        pltpu.make_async_copy(sent, sent, bs.at[it, c]).wait()
        for which in range(3):
            across_copy(it, c, which).wait_send()
        for half in range(2):
            core_copy(it, c, row, half, cs, cr).wait_send()
            core_copy(it, c, row_x, half, gs, gr).wait_send()
        return 0

    lax.fori_loop(0, ITERS * CHUNKS, drain, 0)
    lax.fori_loop(0, (ITERS - 1) * CHUNKS, drain_gather, 0)
    for c in range(CHUNKS):
        sent = brecv.at[c, pl.ds(0, (NB - 1) * PORTS)]
        pltpu.make_async_copy(sent, sent, bs.at[ITERS - 1, c]).wait()
        for half in range(2):
            old_copy(c, half).wait()
        last_copy(c).wait()


def body(impedance, excitation, port_gain, port_class, class_limit, harmonic):
    sems, gather = (ITERS, CHUNKS), (ITERS - 1, CHUNKS)
    shape = (2, QUARTER, CHUNKS * LANES)
    old, last = pl.pallas_call(
        kernel,
        name="harmonic_balance",
        out_shape=[jax.ShapeDtypeStruct(shape, F32), jax.ShapeDtypeStruct(shape, BF16)],
        in_specs=[pl.BlockSpec(memory_space=pl.ANY)] * 6,
        out_specs=[pl.BlockSpec(memory_space=pl.ANY)] * 2,
        scratch_shapes=[
            pltpu.VMEM((1, NB), jnp.int32),
            pltpu.SMEM((QUARTER,), F32),
            pltpu.SMEM((QUARTER,), jnp.int32),
            pltpu.SMEM((4,), jnp.int32),
            pltpu.VMEM((2, QUARTER, 4 * QUARTER), BF16),
            pltpu.VMEM(shape, BF16),
            pltpu.VMEM((CHUNKS, 2, QUARTER, LANES), BF16),
            pltpu.VMEM(sems + (QUARTER, 2, LANES), BF16),
            pltpu.VMEM(sems + (PORTS, NB, 2, LANES), BF16),
            pltpu.VMEM(sems + (2, PORTS, PLANE, 2, LANES), BF16),
            pltpu.VMEM(gather + (2, HALF, 2, LANES), BF16),
            pltpu.VMEM((CHUNKS, QUARTER, 2, LANES), BF16),
            pltpu.VMEM(gather + (3, HALF, 2, LANES), BF16),
            pltpu.VMEM(gather + (4, QUARTER, 2 * LANES), BF16),
            pltpu.VMEM((CHUNKS, 2, QUARTER, 2 * LANES), F32),
            pltpu.VMEM((2, SAMPLES, SAMPLES), BF16),
            pltpu.VMEM((256, 256), BF16),
            pltpu.VMEM((128, 128), BF16),
            pltpu.VMEM((2, QUARTER, 2 * LANES), F32),
            pltpu.SemaphoreType.DMA((6,)),
            pltpu.SemaphoreType.DMA((CHUNKS, 3)),
            pltpu.SemaphoreType.DMA(sems),
            pltpu.SemaphoreType.DMA(sems),
            pltpu.SemaphoreType.DMA(sems),
            pltpu.SemaphoreType.DMA((CHUNKS,)),
            pltpu.SemaphoreType.DMA(gather),
            pltpu.SemaphoreType.DMA(gather + (3,)),
            pltpu.SemaphoreType.DMA(gather + (3,)),
        ]
        + [pltpu.SemaphoreType.DMA(gather + (2,))] * 4,
        compiler_params=pltpu.CompilerParams(
            collective_id=0, has_side_effects=True, vmem_limit_bytes=60 << 20
        ),
    )(
        harmonic.reshape(1, NB),
        port_gain,
        port_class,
        class_limit,
        impedance.reshape(2, QUARTER, 4 * QUARTER),
        excitation.reshape(2, QUARTER, CHUNKS * LANES),
    )
    new = old + RELAXATION * (last.astype(F32) - old)
    return new.reshape(excitation.shape)


def solution(mesh):
    placed = (
        P(None, "band", "row", None),
        P(None, "band", "row", None),
        P("row"),
        P("row"),
        P(),
        P(),
    )
    return jax.shard_map(
        body, mesh=mesh, in_specs=placed, out_specs=P(None, "band", "row", None), check_vma=False
    )
```
